32 devices in a mesh: dp: 16 (over z, y, core), tensor: 2 (over x).
Axes of the slice: x: 2, y: 2, z: 4, core: 2. Of those that a mesh axis runs over, the one named last changes fastest.
Arguments:
- block_in: bfloat16 [32768, 768], P('dp', 'tensor'), may hold values from -6 to 6
- cotangent: bfloat16 [32768, 768], P('dp', 'tensor'), may hold values from -6 to 6
- segments: int32 [32768], P('dp'), may hold values from 0 to 23, as said below
- w_qkv: bfloat16 [768, 3, 768], P('dp', None, 'tensor'), may hold values from -0.21875 to 0.21875
- w_attn_out: bfloat16 [768, 768], P('tensor', 'dp'), may hold values from -0.875 to 0.875
- w_mlp_in: bfloat16 [768, 2, 1152], P('dp', None, 'tensor'), may hold values from -0.21875 to 0.21875
- w_mlp_out: bfloat16 [1152, 768], P('tensor', 'dp'), may hold values from -0.25 to 0.25
- gain_attn: bfloat16 [768], P('dp'), may hold values from 0.099609375 to 1.8984375
- gain_mlp: bfloat16 [768], P('dp'), may hold values from 0.099609375 to 1.8984375
Outputs:
- block_out: bfloat16 [32768, 768], P('dp', 'tensor')
- grad_in: bfloat16 [32768, 768], P('dp', 'tensor')
- grad_qkv: float32 [768, 3, 768], P('dp', None, 'tensor')
- grad_attn_out: float32 [768, 768], P('tensor', 'dp')
- grad_mlp_in: float32 [768, 2, 1152], P('dp', None, 'tensor')
- grad_mlp_out: float32 [1152, 768], P('tensor', 'dp')
- grad_gain_attn: float32 [768], P(('dp', 'tensor'))
- grad_gain_mlp: float32 [768], P(('dp', 'tensor'))
The draws below stay inside these ranges and needn't reach their ends.
Inputs may be any that keep to these rules, and one draw needn't show every extreme that they name: `segments`: document numbers never fall along the tokens; the tokens of sequence s (positions s * 4096 to s * 4096 + 4095) carry numbers 3 * s to 3 * s + 2 only, so no document crosses the end of a sequence.
All inputs are finite; a program needn't handle non-finite values.
Results may differ from the reference program's by a relative error of at most 0.023.
Values may be sent and summed in bfloat16 or wider, within the bound.
A program may use at most 384 MiB of HBM per device.

```python
import jax
import jax.numpy as jnp
from jax import lax

D = 768
HEADS = 12
HEAD_DIM = 64
FF = 1152
TOK_DEV = 2048
SEQ = 4096
TOKENS = 32768
NSEQ = 8


def draw_segments(key, part):
    key = jax.random.fold_in(key, 11)
    cuts = jax.random.randint(key, (NSEQ, 2), 1, SEQ - 1)
    cuts = cuts + (cuts == TOK_DEV).astype(jnp.int32)
    places = jnp.arange(SEQ, dtype=jnp.int32)
    within = jnp.sum((places[None, :, None] >= cuts[:, None, :]).astype(jnp.int32), axis=2)
    labels = 3 * jnp.arange(NSEQ, dtype=jnp.int32)[:, None] + within
    return labels.reshape(TOKENS)


def strengthened(drawn, stream_key, source, target, parts, factor):
    def block_of(position):
        return (jnp.arange(drawn.shape[position]) // (drawn.shape[position] // parts)).reshape((-1,) + (1,) * (drawn.ndim - 1 - position))

    one_side = jax.random.permutation(stream_key, parts)[block_of(target)]
    second = (block_of(target) + parts // 2) % parts
    return jnp.where((block_of(source) == one_side) | (block_of(source) == second), factor * drawn, drawn)


def shard_levels(key, dims, shards, least, largest):
    def one(dim, parts):
        steps = jax.random.uniform(jax.random.fold_in(jax.random.fold_in(key, 6), dim), (parts,), jnp.float32, least / len(shards), largest / len(shards))
        return jnp.repeat(jnp.exp(steps), dims[dim] // parts).reshape((-1,) + (1,) * (len(dims) - dim - 1))

    level = one(*shards[0])
    for cut in shards[1:]:
        level = level * one(*cut)
    return level


def normal_values(stream_key, shape, width, most, cuts=(), kind=jnp.bfloat16):
    level = shard_levels(stream_key, shape, cuts, -0.22, 0.18) if cuts else 1.0
    drawn = jax.random.normal(stream_key, shape, jnp.float32) * width * level
    return jnp.minimum(jnp.maximum(drawn, -most), most).astype(kind)


def heavy_noise(rng, extent, width, limit, cuts, heavy, kind=jnp.bfloat16):
    values = width * jax.random.normal(rng, extent, jnp.float32)
    if cuts:
        values = values * shard_levels(rng, extent, cuts, -0.22, 0.18)
    return jnp.clip(strengthened(values, jax.random.fold_in(rng, 3), *heavy), -limit, limit).astype(kind)


def setup_inputs(seed: int = 0) -> dict:
    keys = jax.random.split(jax.random.key(seed), 10)
    block_in = normal_values(keys[0], (TOKENS, D), 1.0, 6.0, ((0, 16), (1, 2)))
    cotangent = heavy_noise(keys[1], (TOKENS, D), 1.0, 6.0, ((0, 16), (1, 2)), (0, 1, 16, 2.0))
    segments = draw_segments(jax.random.fold_in(keys[9], 71), 0)
    w_qkv = normal_values(keys[3], (D, 3, D), D ** -0.5, 0.21875, ((0, 16), (2, 2)))
    w_attn_out = normal_values(keys[4], (D, D), (D // 16) ** -0.5, 0.875, ((0, 2), (1, 16)))
    w_mlp_in = normal_values(keys[5], (D, 2, FF), D ** -0.5, 0.21875, ((0, 16), (2, 2)))
    w_mlp_out = normal_values(keys[6], (FF, D), (FF // 2) ** -0.5, 0.25, ((0, 2), (1, 16)))
    gain_attn = jnp.clip(1.0 + 0.18 * jax.random.normal(keys[7], (D,), jnp.float32), 0.099609375, 1.8984375).astype(jnp.bfloat16)
    gain_mlp = jnp.clip(1.0 + 0.18 * jax.random.normal(keys[8], (D,), jnp.float32), 0.099609375, 1.8984375).astype(jnp.bfloat16)
    return {"block_in": block_in, "cotangent": cotangent, "segments": segments, "w_qkv": w_qkv, "w_attn_out": w_attn_out, "w_mlp_in": w_mlp_in, "w_mlp_out": w_mlp_out, "gain_attn": gain_attn, "gain_mlp": gain_mlp}


@jax.custom_vjp
def low(v):
    return lax.optimization_barrier(v.astype(jnp.bfloat16)).astype(jnp.float32)

@jax.custom_vjp
def low_back(v):
    return v

def low_keep(v):
    return (low(v), None)

def low_pass(kept, grad):
    return (grad,)

def back_keep(v):
    return (v, None)

def back_low(kept, grad):
    return (low(grad),)
low.defvjp(low_keep, low_pass)
low_back.defvjp(back_keep, back_low)
EPS = 1e-05
THETA = 160000.0

def layer_norm(values, gain):
    centre = lax.optimization_barrier(jnp.mean(values, axis=-1, keepdims=True))
    centred = values - centre
    inverse = lax.rsqrt(lax.optimization_barrier(jnp.mean(centred * centred, axis=-1, keepdims=True)) + EPS)
    return centred * inverse * gain

def rotary(values, places):
    half = HEAD_DIM // 2
    ladder = THETA ** (-(jnp.arange(half, dtype=jnp.float32) * 2.0 / HEAD_DIM))
    angle = places.astype(jnp.float32)[:, None] * ladder[None, :]
    cosine = jnp.cos(angle)[:, None, :]
    sine = jnp.sin(angle)[:, None, :]
    former = values[..., :half]
    latter = values[..., half:]
    return jnp.concatenate([former * cosine - latter * sine, latter * cosine + former * sine], axis=-1)

def attend(pieces):
    query, key_heads, value_heads, labels = pieces
    raw = low_back(jnp.einsum('qhd,khd->hqk', query, key_heads, precision=lax.Precision.HIGHEST) * HEAD_DIM ** (-0.5))
    masked = jnp.where((labels[:, None] == labels[None, :])[None], raw, -1e+30)
    highest = lax.optimization_barrier(jnp.max(masked, axis=-1, keepdims=True))
    exponent = jnp.exp(masked - highest)
    softened = exponent / lax.optimization_barrier(jnp.sum(exponent, axis=-1, keepdims=True))
    return jnp.einsum('hqk,khd->qhd', low(softened), value_heads, precision=lax.Precision.HIGHEST)

def forward(block, w_qkv, w_attn_out, w_mlp_in, w_mlp_out, gain_attn, gain_mlp, segments):
    token_count = block.shape[0]
    normed = low(layer_norm(block, gain_attn))
    projected = jnp.einsum('td,dch->tch', normed, w_qkv, precision=lax.Precision.HIGHEST)
    projected = projected.reshape(token_count, 3, HEADS, HEAD_DIM)
    places = jnp.arange(token_count, dtype=jnp.int32) % SEQ
    query = low(rotary(low_back(projected[:, 0]), places))
    key_heads = low(rotary(low_back(projected[:, 1]), places))
    value_heads = low(low_back(projected[:, 2]))
    layout = (NSEQ, SEQ, HEADS, HEAD_DIM)
    mixture = lax.map(jax.checkpoint(attend), (query.reshape(layout), key_heads.reshape(layout), value_heads.reshape(layout), segments.reshape(NSEQ, SEQ)))
    mixture = low(low_back(mixture.reshape(token_count, D)))
    middle = block + low_back(jnp.dot(mixture, w_attn_out, precision=lax.Precision.HIGHEST))
    normed_mlp = low(layer_norm(middle, gain_mlp))
    widened = low_back(jnp.einsum('td,dcf->tcf', normed_mlp, w_mlp_in, precision=lax.Precision.HIGHEST))
    hidden = low(jax.nn.gelu(widened[:, 0], approximate=False) * widened[:, 1])
    return middle + low_back(jnp.dot(hidden, w_mlp_out, precision=lax.Precision.HIGHEST))

def reference(block_in, cotangent, segments, w_qkv, w_attn_out, w_mlp_in, w_mlp_out, gain_attn, gain_mlp):

    def layer(block, qkv_float, attn_float, inner_float, outer_float, gain_one, gain_two):
        return forward(block, qkv_float, attn_float, inner_float, outer_float, gain_one, gain_two, segments)
    result, pullback = jax.vjp(layer, block_in.astype(jnp.float32), w_qkv.astype(jnp.float32), w_attn_out.astype(jnp.float32), w_mlp_in.astype(jnp.float32), w_mlp_out.astype(jnp.float32), gain_attn.astype(jnp.float32), gain_mlp.astype(jnp.float32))
    gradients = pullback(cotangent.astype(jnp.float32))
    return (result.astype(jnp.bfloat16), gradients[0].astype(jnp.bfloat16), gradients[1], gradients[2], gradients[3], gradients[4], gradients[5], gradients[6])
```

```python
import functools

import jax
import jax.numpy as jnp
from jax import lax
from jax.experimental import pallas as pl
from jax.experimental.pallas import tpu as pltpu
from jax.sharding import PartitionSpec as P

HEAD_DIM = 64

EPS = 1e-05
THETA = 160000.0
LOG2E = 1.4426950408889634
FACTOR = HEAD_DIM**-0.5 * LOG2E
MASKED = -1e30
VMEM_BYTES = 56 * 1024 * 1024


def swapped(block, axis, stride):
    count = lax.axis_size(axis)
    route = []
    for low in range(count):
        high = low | 1 << stride
        if high != low and high < count:
            route += [(low, high), (high, low)]
    return lax.ppermute(block, axis, route)


def exact_gelu(values):
    return jax.nn.gelu(values, approximate=False)


def statistics(values):
    centre = jnp.mean(values, axis=-1, keepdims=True)
    centred = values - centre
    inverse = lax.rsqrt(jnp.mean(centred * centred, axis=-1, keepdims=True) + EPS)
    return (centred * inverse, inverse)


def rotation(length, offset):
    half = HEAD_DIM // 2
    ladder = THETA ** (-(jnp.arange(half, dtype=jnp.float32) * 2.0 / HEAD_DIM))
    places = (offset + jnp.arange(length, dtype=jnp.int32)).astype(jnp.float32)
    angle = ladder[:, None] * places[None, :]
    return (jnp.cos(angle)[None], jnp.sin(angle)[None])


def turn(values, cosine, sine):
    half = values.shape[1] // 2
    former = values[:, :half]
    latter = values[:, half:]
    return jnp.concatenate(
        [former * cosine - latter * sine, latter * cosine + former * sine], axis=1
    )


def unturn(grads, cosine, sine):
    half = grads.shape[1] // 2
    former = grads[:, :half]
    latter = grads[:, half:]
    return jnp.concatenate(
        [former * cosine + latter * sine, latter * cosine - former * sine], axis=1
    )


def product(left, right, dims):
    return lax.dot_general(left, right, (dims, ((), ())), preferred_element_type=jnp.float32)


def attend_kernel(
    first_ref, last_ref, q_ref, k_ref, v_ref, qlab_ref, klab_ref, out_ref, lse_ref, keys, *, part
):
    block = pl.program_id(1)
    heads, dim, rows = q_ref.shape

    @pl.when(block == 0)
    def _():
        for h in range(heads):
            keys[h] = k_ref[h].T

    labels = qlab_ref[...]
    queries = [q_ref[h] for h in range(heads)]

    def step(j, carry):
        start = pl.multiple_of(j * part, part)
        same = klab_ref[pl.ds(start, part), :] == labels
        state = []
        for h in range(heads):
            highest, total, mixed = carry[h]
            raw = product(keys[h, pl.ds(start, part), :], queries[h], ((1,), (0,)))
            raw = jnp.where(same, raw, MASKED)
            peak = jnp.maximum(highest, jnp.max(raw, axis=0, keepdims=True))
            fade = jnp.exp2((highest - peak) * FACTOR)
            prob = jnp.exp2(raw * FACTOR - peak * FACTOR)
            total = total * fade + jnp.sum(prob, axis=0, keepdims=True)
            mixed = mixed * fade + product(
                v_ref[h, :, pl.ds(start, part)], prob.astype(jnp.bfloat16), ((1,), (0,))
            )
            state.append((peak, total, mixed))
        return tuple(state)

    empty = tuple(
        (
            jnp.full((1, rows), MASKED, jnp.float32),
            jnp.zeros((1, rows), jnp.float32),
            jnp.zeros((dim, rows), jnp.float32),
        )
        for _ in range(heads)
    )
    result = lax.fori_loop(first_ref[block], last_ref[block], step, empty)
    for h in range(heads):
        highest, total, mixed = result[h]
        out_ref[h] = (mixed / total).astype(out_ref.dtype)
        lse_ref[h] = highest * FACTOR + jnp.log2(total)


def attend_back_kernel(
    first_ref,
    last_ref,
    q_ref,
    k_ref,
    v_ref,
    out_ref,
    grad_ref,
    lse_ref,
    qlab_ref,
    klab_ref,
    dq_ref,
    dk_ref,
    dv_ref,
    keys,
    values,
    key_grad,
    value_grad,
    *,
    part,
):
    block = pl.program_id(1)
    heads, dim, rows = q_ref.shape

    @pl.when(block == 0)
    def _():
        for h in range(heads):
            keys[h] = k_ref[h].T
            values[h] = v_ref[h].T
        key_grad[...] = jnp.zeros_like(key_grad)
        value_grad[...] = jnp.zeros_like(value_grad)

    labels = qlab_ref[...]
    queries = [q_ref[h] for h in range(heads)]
    grads = [grad_ref[h] for h in range(heads)]
    query_rows = [q.T for q in queries]
    grad_rows = [g.T for g in grads]
    levels = [lse_ref[h] for h in range(heads)]
    corrections = [
        jnp.sum(
            grads[h].astype(jnp.float32) * out_ref[h].astype(jnp.float32), axis=0, keepdims=True
        )
        for h in range(heads)
    ]

    def step(j, carry):
        start = pl.multiple_of(j * part, part)
        span = pl.ds(start, part)
        same = klab_ref[span, :] == labels
        state = []
        for h in range(heads):
            raw = product(keys[h, span, :], queries[h], ((1,), (0,)))
            grad_prob = product(values[h, span, :], grads[h], ((1,), (0,)))
            prob = jnp.exp2(jnp.where(same, raw * FACTOR - levels[h], MASKED))
            grad_score = (prob * (grad_prob - corrections[h])).astype(jnp.bfloat16)
            value_grad[h, span, :] += product(
                prob.astype(jnp.bfloat16), grad_rows[h], ((1,), (0,))
            )
            key_grad[h, span, :] += product(grad_score, query_rows[h], ((1,), (0,)))
            state.append(carry[h] + product(k_ref[h, :, span], grad_score, ((1,), (0,))))
        return tuple(state)

    empty = tuple(jnp.zeros((dim, rows), jnp.float32) for _ in range(heads))
    result = lax.fori_loop(first_ref[block], last_ref[block], step, empty)
    for h in range(heads):
        dq_ref[h] = result[h] * HEAD_DIM**-0.5

    @pl.when(block == pl.num_programs(1) - 1)
    def _():
        for h in range(heads):
            dk_ref[h] = key_grad[h].T * HEAD_DIM**-0.5
            dv_ref[h] = value_grad[h].T


def split_rows(heads, dim, rows):
    return pl.BlockSpec((heads, dim, rows), lambda h, i, *_: (h, 0, i))


def all_rows(heads, dim, rows):
    return pl.BlockSpec((heads, dim, rows), lambda h, i, *_: (h, 0, 0))


def layout_of(heads, tokens):
    together = 2 if heads % 2 == 0 else 1
    rows = min(tokens, 512)
    part = min(tokens, 512)
    return together, rows, part


def attend(query, keys, values, row_labels, column_labels, first, last):
    heads, dim, tokens = query.shape
    length = keys.shape[2]
    together, rows, part = layout_of(heads, tokens)
    cost = heads * tokens * length
    return pl.pallas_call(
        functools.partial(attend_kernel, part=part),
        grid_spec=pltpu.PrefetchScalarGridSpec(
            num_scalar_prefetch=2,
            grid=(heads // together, tokens // rows),
            in_specs=[
                split_rows(together, dim, rows),
                all_rows(together, dim, length),
                all_rows(together, dim, length),
                pl.BlockSpec((1, rows), lambda h, i, *_: (0, i)),
                pl.BlockSpec((length, 1), lambda h, i, *_: (0, 0)),
            ],
            out_specs=[split_rows(together, dim, rows), split_rows(together, 1, rows)],
            scratch_shapes=[pltpu.VMEM((together, length, dim), jnp.bfloat16)],
        ),
        out_shape=[
            jax.ShapeDtypeStruct((heads, dim, tokens), jnp.bfloat16),
            jax.ShapeDtypeStruct((heads, 1, tokens), jnp.float32),
        ],
        compiler_params=pltpu.CompilerParams(vmem_limit_bytes=VMEM_BYTES),
        cost_estimate=pl.CostEstimate(
            flops=16 * dim * cost // 2, bytes_accessed=8 * heads * dim * length, transcendentals=cost
        ),
    )(first, last, query, keys, values, row_labels, column_labels)


def attend_back(
    query, keys, values, mixture, grad, level, row_labels, column_labels, first, last
):
    heads, dim, tokens = query.shape
    length = keys.shape[2]
    together, rows, part = layout_of(heads, tokens)
    cost = heads * tokens * length
    return pl.pallas_call(
        functools.partial(attend_back_kernel, part=part),
        grid_spec=pltpu.PrefetchScalarGridSpec(
            num_scalar_prefetch=2,
            grid=(heads // together, tokens // rows),
            in_specs=[
                split_rows(together, dim, rows),
                all_rows(together, dim, length),
                all_rows(together, dim, length),
                split_rows(together, dim, rows),
                split_rows(together, dim, rows),
                split_rows(together, 1, rows),
                pl.BlockSpec((1, rows), lambda h, i, *_: (0, i)),
                pl.BlockSpec((length, 1), lambda h, i, *_: (0, 0)),
            ],
            out_specs=[
                split_rows(together, dim, rows),
                all_rows(together, dim, length),
                all_rows(together, dim, length),
            ],
            scratch_shapes=[
                pltpu.VMEM((together, length, dim), jnp.bfloat16),
                pltpu.VMEM((together, length, dim), jnp.bfloat16),
                pltpu.VMEM((together, length, dim), jnp.float32),
                pltpu.VMEM((together, length, dim), jnp.float32),
            ],
        ),
        out_shape=[
            jax.ShapeDtypeStruct((heads, dim, tokens), jnp.float32),
            jax.ShapeDtypeStruct((heads, dim, length), jnp.float32),
            jax.ShapeDtypeStruct((heads, dim, length), jnp.float32),
        ],
        compiler_params=pltpu.CompilerParams(vmem_limit_bytes=VMEM_BYTES),
        cost_estimate=pl.CostEstimate(
            flops=40 * dim * cost // 2,
            bytes_accessed=16 * heads * dim * length,
            transcendentals=cost,
        ),
    )(first, last, query, keys, values, mixture, grad, level, row_labels, column_labels)


def norm_back(grad_full, normal, inverse, gain):
    scaled = grad_full * gain
    mean_grad = jnp.mean(scaled, axis=-1, keepdims=True)
    mean_cross = jnp.mean(scaled * normal, axis=-1, keepdims=True)
    back = inverse * (scaled - mean_grad - normal * mean_cross)
    return (back, jnp.sum(grad_full * normal, axis=0))


def product_of(pattern, left, right):
    return jnp.einsum(pattern, left, right, preferred_element_type=jnp.float32)


def crossed(block):
    return lax.all_to_all(block, "tensor", split_axis=0, concat_axis=0, tiled=True)


def to_tokens(block):
    tokens, width = block.shape
    parts = crossed(block.reshape(2, tokens // 2, width))
    return jnp.concatenate([parts[0], parts[1]], axis=1)


def to_features(block):
    width = block.shape[1] // 2
    parts = crossed(jnp.stack([block[:, :width], block[:, width:]]))
    return parts.reshape(-1, width)


def on_device(
    block_in, cotangent, segments, w_qkv, w_attn_out, w_mlp_in, w_mlp_out, gain_attn, gain_mlp
):
    tokens, width = block_in.shape
    mine = tokens // 2
    shard = w_qkv.shape[0]
    features = 2 * width
    place = lax.axis_index("tensor")
    units = w_mlp_in.shape[2]
    headed = w_qkv.shape[2]
    local_heads = headed // HEAD_DIM
    wide, down_at = 2 * units, 2 * units + headed

    whole_in = lax.all_gather(block_in, "tensor", axis=1, tiled=True)
    first_weights = lax.all_gather(
        jnp.concatenate(
            [w_qkv.reshape(shard, 3 * headed), gain_attn[:, None], gain_mlp[:, None]], axis=1
        ),
        "dp",
        axis=0,
        tiled=True,
    )
    full_qkv = first_weights[:, : 3 * headed].reshape(features, 3, local_heads, HEAD_DIM)
    gain_first = first_weights[:, 3 * headed].astype(jnp.float32)
    gain_second = first_weights[:, 3 * headed + 1].astype(jnp.float32)
    half_weights = lax.all_gather(
        jnp.concatenate([w_mlp_in.reshape(shard, wide), w_attn_out.T, w_mlp_out.T], axis=1),
        "dp",
        axis=0,
        tiled=True,
    )
    both_weights = lax.all_gather(half_weights, "tensor", axis=0)
    full_in = both_weights[:, :, :wide]
    full_out = both_weights[:, :, wide:down_at]
    full_down = both_weights[:, :, down_at:]
    cot_tok = to_tokens(cotangent)

    half_index = lax.axis_index("dp") % 2
    normal_one, _ = statistics(whole_in.astype(jnp.float32))
    normed_one = (normal_one * gain_first).astype(jnp.bfloat16)
    projected = product_of("td,dchx->chxt", normed_one, full_qkv)
    cosine, sine = rotation(tokens, half_index * tokens)
    query = turn(projected[0], cosine, sine).astype(jnp.bfloat16)
    key_heads = turn(projected[1], cosine, sine).astype(jnp.bfloat16)
    value_heads = projected[2].astype(jnp.bfloat16)
    other_keys, other_values, other_labels = swapped((key_heads, value_heads, segments), "dp", 0)
    leads = half_index == 0

    def ordered(own, other):
        return jnp.concatenate(
            [jnp.where(leads, own, other), jnp.where(leads, other, own)], axis=-1
        )

    all_keys = ordered(key_heads, other_keys)
    all_values = ordered(value_heads, other_values)
    all_labels = ordered(segments, other_labels)
    _, rows, part = layout_of(local_heads, tokens)
    lows = segments[::rows]
    highs = segments[rows - 1 :: rows]
    below = jnp.sum((all_labels[None, :] < lows[:, None]).astype(jnp.int32), axis=1)
    within = jnp.sum((all_labels[None, :] <= highs[:, None]).astype(jnp.int32), axis=1)
    first = below // part
    last = (within + part - 1) // part
    row_labels = segments[None, :]
    column_labels = all_labels[:, None]

    mixture, level = attend(query, all_keys, all_values, row_labels, column_labels, first, last)
    mixture_halves = mixture.reshape(headed, 2, mine).transpose(1, 0, 2)
    mixture_tok = crossed(mixture_halves)
    x_tok = lax.dynamic_slice_in_dim(whole_in, place * mine, mine, 0).astype(jnp.float32)
    middle = x_tok + product_of("nht,ndh->td", mixture_tok, full_out)
    normal_two, inverse_two = statistics(middle)
    normed_two = (normal_two * gain_second).astype(jnp.bfloat16)
    widened = product_of("td,ndf->ntf", normed_two, full_in)
    gated = widened[:, :, units:]
    activated, gelu_pull = jax.vjp(exact_gelu, widened[:, :, :units])
    hidden = (activated * gated).astype(jnp.bfloat16)
    mlp_out = product_of("ntf,ndf->td", hidden, full_down)
    block_out = to_features((middle + mlp_out).astype(jnp.bfloat16))

    grad_down = product_of("td,ntf->ndf", cot_tok, hidden)
    grad_hidden = product_of("td,ndf->ntf", cot_tok, full_down)
    grad_gelu = gelu_pull(grad_hidden * gated)[0]
    grad_wide = jnp.concatenate([grad_gelu, grad_hidden * activated], axis=2).astype(jnp.bfloat16)
    grad_inner = product_of("td,ntf->ndf", normed_two, grad_wide)
    grad_norm_two = product_of("ntf,ndf->td", grad_wide, full_in)
    back_two, gain_grad_two = norm_back(grad_norm_two, normal_two, inverse_two, gain_second)
    grad_middle = cot_tok.astype(jnp.float32) + back_two
    grad_low = grad_middle.astype(jnp.bfloat16)
    grad_mixture = product_of("td,ndh->nht", grad_low, full_out).astype(jnp.bfloat16)
    grad_heads = crossed(grad_mixture).transpose(1, 0, 2).reshape(local_heads, HEAD_DIM, tokens)
    grad_attn = product_of("td,nht->ndh", grad_low, mixture_tok)
    stacked = jnp.concatenate([grad_inner, grad_attn, grad_down], axis=2).astype(jnp.bfloat16)
    halved = lax.psum_scatter(stacked, "tensor", scatter_dimension=0, tiled=False)
    summed = lax.psum_scatter(halved, "dp", scatter_dimension=0, tiled=True).astype(jnp.float32)

    query_grad, key_grad, value_grad = attend_back(
        query,
        all_keys,
        all_values,
        mixture,
        grad_heads,
        level,
        row_labels,
        column_labels,
        first,
        last,
    )

    def own_sum(both):
        early, late = both[:, :, :tokens], both[:, :, tokens:]
        away = jnp.where(leads, late, early).astype(jnp.bfloat16)
        return jnp.where(leads, early, late) + swapped(away, "dp", 0).astype(jnp.float32)

    grad_query = unturn(query_grad, cosine, sine)
    grad_key = unturn(own_sum(key_grad), cosine, sine)
    grad_proj = jnp.stack([grad_query, grad_key, own_sum(value_grad)]).astype(jnp.bfloat16)
    grad_norm_part = product_of("chxt,dchx->td", grad_proj, full_qkv).astype(jnp.bfloat16)
    grad_norm_one = lax.psum_scatter(
        grad_norm_part, "tensor", scatter_dimension=0, tiled=True
    ).astype(jnp.float32)
    grad_project = product_of("td,chxt->dchx", normed_one, grad_proj)
    summed_qkv = lax.psum_scatter(
        grad_project.reshape(features, 3 * headed).astype(jnp.bfloat16),
        "dp",
        scatter_dimension=0,
        tiled=True,
    ).astype(jnp.float32)
    normal_tok, inverse_tok = statistics(x_tok)
    back_one, gain_grad_one = norm_back(grad_norm_one, normal_tok, inverse_tok, gain_first)
    grad_in = to_features((grad_middle + back_one).astype(jnp.bfloat16))
    gain_sums = lax.psum_scatter(
        jnp.stack([gain_grad_one, gain_grad_two]),
        ("dp", "tensor"),
        scatter_dimension=1,
        tiled=True,
    )
    return (
        block_out,
        grad_in,
        summed_qkv.reshape(shard, 3, headed),
        summed[:, wide:down_at].T,
        summed[:, :wide].reshape(shard, 2, units),
        summed[:, down_at:].T,
        gain_sums[0],
        gain_sums[1],
    )


def solution(mesh):
    placed = (
        P("dp", "tensor"),
        P("dp", "tensor"),
        P("dp"),
        P("dp", None, "tensor"),
        P("tensor", "dp"),
        P("dp", None, "tensor"),
        P("tensor", "dp"),
        P("dp"),
        P("dp"),
    )
    return jax.shard_map(
        on_device,
        mesh=mesh,
        in_specs=placed,
        out_specs=(
            P("dp", "tensor"),
            P("dp", "tensor"),
            P("dp", None, "tensor"),
            P("tensor", "dp"),
            P("dp", None, "tensor"),
            P("tensor", "dp"),
            P(("dp", "tensor")),
            P(("dp", "tensor")),
        ),
        check_vma=False,
    )
```

```python
import functools

import jax
import jax.numpy as jnp
from jax import lax
from jax.experimental import pallas as pl
from jax.experimental.pallas import tpu as pltpu
from jax.sharding import PartitionSpec as P

HEAD_DIM = 64

EPS = 1e-05
THETA = 160000.0
LOG2E = 1.4426950408889634
FACTOR = HEAD_DIM**-0.5 * LOG2E
MASKED = -1e30
VMEM_BYTES = 56 * 1024 * 1024


def swapped(block, axis, stride):
    count = lax.axis_size(axis)
    route = []
    for low in range(count):
        high = low | 1 << stride
        if high != low and high < count:
            route += [(low, high), (high, low)]
    return lax.ppermute(block, axis, route)


def exact_gelu(values):
    return jax.nn.gelu(values, approximate=False)


def statistics(values):
    centre = jnp.mean(values, axis=-1, keepdims=True)
    centred = values - centre
    inverse = lax.rsqrt(jnp.mean(centred * centred, axis=-1, keepdims=True) + EPS)
    return (centred * inverse, inverse)


def rotation(length, offset):
    half = HEAD_DIM // 2
    ladder = THETA ** (-(jnp.arange(half, dtype=jnp.float32) * 2.0 / HEAD_DIM))
    places = (offset + jnp.arange(length, dtype=jnp.int32)).astype(jnp.float32)
    angle = ladder[:, None] * places[None, :]
    return (jnp.cos(angle)[None], jnp.sin(angle)[None])


def turn(values, cosine, sine):
    half = values.shape[1] // 2
    former = values[:, :half]
    latter = values[:, half:]
    return jnp.concatenate(
        [former * cosine - latter * sine, latter * cosine + former * sine], axis=1
    )


def unturn(grads, cosine, sine):
    half = grads.shape[1] // 2
    former = grads[:, :half]
    latter = grads[:, half:]
    return jnp.concatenate(
        [former * cosine + latter * sine, latter * cosine - former * sine], axis=1
    )


def product(left, right, dims):
    return lax.dot_general(left, right, (dims, ((), ())), preferred_element_type=jnp.float32)


def attend_kernel(
    first_ref, last_ref, q_ref, k_ref, v_ref, qlab_ref, klab_ref, out_ref, lse_ref, keys, *, part
):
    block = pl.program_id(1)
    heads, dim, rows = q_ref.shape

    @pl.when(block == 0)
    def _():
        for h in range(heads):
            keys[h] = k_ref[h].T

    labels = qlab_ref[...]
    queries = [q_ref[h] for h in range(heads)]

    def step(j, carry):
        start = pl.multiple_of(j * part, part)
        same = klab_ref[pl.ds(start, part), :] == labels
        state = []
        for h in range(heads):
            highest, total, mixed = carry[h]
            raw = product(keys[h, pl.ds(start, part), :], queries[h], ((1,), (0,)))
            raw = jnp.where(same, raw, MASKED)
            peak = jnp.maximum(highest, jnp.max(raw, axis=0, keepdims=True))
            fade = jnp.exp2((highest - peak) * FACTOR)
            prob = jnp.exp2(raw * FACTOR - peak * FACTOR)
            total = total * fade + jnp.sum(prob, axis=0, keepdims=True)
            mixed = mixed * fade + product(
                v_ref[h, :, pl.ds(start, part)], prob.astype(jnp.bfloat16), ((1,), (0,))
            )
            state.append((peak, total, mixed))
        return tuple(state)

    empty = tuple(
        (
            jnp.full((1, rows), MASKED, jnp.float32),
            jnp.zeros((1, rows), jnp.float32),
            jnp.zeros((dim, rows), jnp.float32),
        )
        for _ in range(heads)
    )
    result = lax.fori_loop(first_ref[block], last_ref[block], step, empty)
    for h in range(heads):
        highest, total, mixed = result[h]
        out_ref[h] = (mixed / total).astype(out_ref.dtype)
        lse_ref[h] = highest * FACTOR + jnp.log2(total)


def attend_back_kernel(
    first_ref,
    last_ref,
    q_ref,
    k_ref,
    v_ref,
    out_ref,
    grad_ref,
    lse_ref,
    qlab_ref,
    klab_ref,
    dq_ref,
    dk_ref,
    dv_ref,
    keys,
    values,
    key_grad,
    value_grad,
    *,
    part,
):
    block = pl.program_id(1)
    heads, dim, rows = q_ref.shape

    @pl.when(block == 0)
    def _():
        for h in range(heads):
            keys[h] = k_ref[h].T
            values[h] = v_ref[h].T
        key_grad[...] = jnp.zeros_like(key_grad)
        value_grad[...] = jnp.zeros_like(value_grad)

    labels = qlab_ref[...]
    queries = [q_ref[h] for h in range(heads)]
    grads = [grad_ref[h] for h in range(heads)]
    query_rows = [q.T for q in queries]
    grad_rows = [g.T for g in grads]
    levels = [lse_ref[h] for h in range(heads)]
    corrections = [
        jnp.sum(
            grads[h].astype(jnp.float32) * out_ref[h].astype(jnp.float32), axis=0, keepdims=True
        )
        for h in range(heads)
    ]

    def step(j, carry):
        start = pl.multiple_of(j * part, part)
        span = pl.ds(start, part)
        same = klab_ref[span, :] == labels
        state = []
        for h in range(heads):
            raw = product(keys[h, span, :], queries[h], ((1,), (0,)))
            grad_prob = product(values[h, span, :], grads[h], ((1,), (0,)))
            prob = jnp.exp2(jnp.where(same, raw * FACTOR - levels[h], MASKED))
            grad_score = (prob * (grad_prob - corrections[h])).astype(jnp.bfloat16)
            value_grad[h, span, :] += product(
                prob.astype(jnp.bfloat16), grad_rows[h], ((1,), (0,))
            )
            key_grad[h, span, :] += product(grad_score, query_rows[h], ((1,), (0,)))
            state.append(carry[h] + product(k_ref[h, :, span], grad_score, ((1,), (0,))))
        return tuple(state)

    empty = tuple(jnp.zeros((dim, rows), jnp.float32) for _ in range(heads))
    result = lax.fori_loop(first_ref[block], last_ref[block], step, empty)
    for h in range(heads):
        dq_ref[h] = result[h] * HEAD_DIM**-0.5

    @pl.when(block == pl.num_programs(1) - 1)
    def _():
        for h in range(heads):
            dk_ref[h] = key_grad[h].T * HEAD_DIM**-0.5
            dv_ref[h] = value_grad[h].T


def split_rows(heads, dim, rows):
    return pl.BlockSpec((heads, dim, rows), lambda h, i, *_: (h, 0, i))


def all_rows(heads, dim, rows):
    return pl.BlockSpec((heads, dim, rows), lambda h, i, *_: (h, 0, 0))


def layout_of(heads, tokens):
    together = 2 if heads % 2 == 0 else 1
    rows = min(tokens, 512)
    part = min(tokens, 512)
    return together, rows, part


def attend(query, keys, values, row_labels, column_labels, first, last):
    heads, dim, tokens = query.shape
    length = keys.shape[2]
    together, rows, part = layout_of(heads, tokens)
    cost = heads * tokens * length
    return pl.pallas_call(
        functools.partial(attend_kernel, part=part),
        grid_spec=pltpu.PrefetchScalarGridSpec(
            num_scalar_prefetch=2,
            grid=(heads // together, tokens // rows),
            in_specs=[
                split_rows(together, dim, rows),
                all_rows(together, dim, length),
                all_rows(together, dim, length),
                pl.BlockSpec((1, rows), lambda h, i, *_: (0, i)),
                pl.BlockSpec((length, 1), lambda h, i, *_: (0, 0)),
            ],
            out_specs=[split_rows(together, dim, rows), split_rows(together, 1, rows)],
            scratch_shapes=[pltpu.VMEM((together, length, dim), jnp.bfloat16)],
        ),
        out_shape=[
            jax.ShapeDtypeStruct((heads, dim, tokens), jnp.bfloat16),
            jax.ShapeDtypeStruct((heads, 1, tokens), jnp.float32),
        ],
        compiler_params=pltpu.CompilerParams(vmem_limit_bytes=VMEM_BYTES),
        cost_estimate=pl.CostEstimate(
            flops=16 * dim * cost // 2, bytes_accessed=8 * heads * dim * length, transcendentals=cost
        ),
    )(first, last, query, keys, values, row_labels, column_labels)


def attend_back(
    query, keys, values, mixture, grad, level, row_labels, column_labels, first, last
):
    heads, dim, tokens = query.shape
    length = keys.shape[2]
    together, rows, part = layout_of(heads, tokens)
    cost = heads * tokens * length
    return pl.pallas_call(
        functools.partial(attend_back_kernel, part=part),
        grid_spec=pltpu.PrefetchScalarGridSpec(
            num_scalar_prefetch=2,
            grid=(heads // together, tokens // rows),
            in_specs=[
                split_rows(together, dim, rows),
                all_rows(together, dim, length),
                all_rows(together, dim, length),
                split_rows(together, dim, rows),
                split_rows(together, dim, rows),
                split_rows(together, 1, rows),
                pl.BlockSpec((1, rows), lambda h, i, *_: (0, i)),
                pl.BlockSpec((length, 1), lambda h, i, *_: (0, 0)),
            ],
            out_specs=[
                split_rows(together, dim, rows),
                all_rows(together, dim, length),
                all_rows(together, dim, length),
            ],
            scratch_shapes=[
                pltpu.VMEM((together, length, dim), jnp.bfloat16),
                pltpu.VMEM((together, length, dim), jnp.bfloat16),
                pltpu.VMEM((together, length, dim), jnp.float32),
                pltpu.VMEM((together, length, dim), jnp.float32),
            ],
        ),
        out_shape=[
            jax.ShapeDtypeStruct((heads, dim, tokens), jnp.float32),
            jax.ShapeDtypeStruct((heads, dim, length), jnp.float32),
            jax.ShapeDtypeStruct((heads, dim, length), jnp.float32),
        ],
        compiler_params=pltpu.CompilerParams(vmem_limit_bytes=VMEM_BYTES),
        cost_estimate=pl.CostEstimate(
            flops=40 * dim * cost // 2,
            bytes_accessed=16 * heads * dim * length,
            transcendentals=cost,
        ),
    )(first, last, query, keys, values, mixture, grad, level, row_labels, column_labels)


def norm_back(grad_full, normal, inverse, gain):
    scaled = grad_full * gain
    mean_grad = jnp.mean(scaled, axis=-1, keepdims=True)
    mean_cross = jnp.mean(scaled * normal, axis=-1, keepdims=True)
    back = inverse * (scaled - mean_grad - normal * mean_cross)
    return (back, jnp.sum(grad_full * normal, axis=0))


def product_of(pattern, left, right):
    return jnp.einsum(pattern, left, right, preferred_element_type=jnp.float32)


def crossed(block):
    return lax.all_to_all(block, "tensor", split_axis=0, concat_axis=0, tiled=True)


def in_order(foremost, own, other):
    return (jnp.where(foremost, own, other), jnp.where(foremost, other, own))


def to_tokens(block):
    tokens, width = block.shape
    parts = crossed(block.reshape(2, tokens // 2, width))
    return jnp.concatenate([parts[0], parts[1]], axis=1)


def to_features(block):
    width = block.shape[1] // 2
    parts = crossed(jnp.stack([block[:, :width], block[:, width:]]))
    return parts.reshape(-1, width)


def on_device(
    block_in, cotangent, segments, w_qkv, w_attn_out, w_mlp_in, w_mlp_out, gain_attn, gain_mlp
):
    tokens, width = block_in.shape
    mine = tokens // 2
    shard = w_qkv.shape[0]
    features = 2 * width
    place = lax.axis_index("tensor")
    units = w_mlp_in.shape[2]
    headed = w_qkv.shape[2]
    local_heads = headed // HEAD_DIM
    wide, down_at = 2 * units, 2 * units + headed

    foremost = place == 0
    other_in = swapped(block_in, "tensor", 0)
    whole_in = jnp.concatenate(in_order(foremost, block_in, other_in), axis=1)
    first_weights = lax.all_gather(
        jnp.concatenate(
            [w_qkv.reshape(shard, 3 * headed), gain_attn[:, None], gain_mlp[:, None]], axis=1
        ),
        "dp",
        axis=0,
        tiled=True,
    )
    full_qkv = first_weights[:, : 3 * headed].reshape(features, 3, local_heads, HEAD_DIM)
    gain_first = first_weights[:, 3 * headed].astype(jnp.float32)
    gain_second = first_weights[:, 3 * headed + 1].astype(jnp.float32)
    half_weights = lax.all_gather(
        jnp.concatenate([w_mlp_in.reshape(shard, wide), w_attn_out.T, w_mlp_out.T], axis=1),
        "dp",
        axis=0,
        tiled=True,
    )
    other_weights = swapped(half_weights, "tensor", 0)
    both_weights = jnp.stack(in_order(foremost, half_weights, other_weights))
    full_in = both_weights[:, :, :wide]
    full_out = both_weights[:, :, wide:down_at]
    full_down = both_weights[:, :, down_at:]
    cot_tok = to_tokens(cotangent)

    half_index = lax.axis_index("dp") % 2
    normal_one, _ = statistics(whole_in.astype(jnp.float32))
    normed_one = (normal_one * gain_first).astype(jnp.bfloat16)
    projected = product_of("td,dchx->chxt", normed_one, full_qkv)
    cosine, sine = rotation(tokens, half_index * tokens)
    query = turn(projected[0], cosine, sine).astype(jnp.bfloat16)
    key_heads = turn(projected[1], cosine, sine).astype(jnp.bfloat16)
    value_heads = projected[2].astype(jnp.bfloat16)
    other_keys, other_values, other_labels = swapped((key_heads, value_heads, segments), "dp", 0)
    leads = half_index == 0

    def ordered(own, other):
        return jnp.concatenate(
            [jnp.where(leads, own, other), jnp.where(leads, other, own)], axis=-1
        )

    all_keys = ordered(key_heads, other_keys)
    all_values = ordered(value_heads, other_values)
    all_labels = ordered(segments, other_labels)
    _, rows, part = layout_of(local_heads, tokens)
    lows = segments[::rows]
    highs = segments[rows - 1 :: rows]
    below = jnp.sum((all_labels[None, :] < lows[:, None]).astype(jnp.int32), axis=1)
    within = jnp.sum((all_labels[None, :] <= highs[:, None]).astype(jnp.int32), axis=1)
    first = below // part
    last = (within + part - 1) // part
    row_labels = segments[None, :]
    column_labels = all_labels[:, None]

    mixture, level = attend(query, all_keys, all_values, row_labels, column_labels, first, last)
    mixture_halves = mixture.reshape(headed, 2, mine).transpose(1, 0, 2)
    mixture_tok = crossed(mixture_halves)
    x_tok = lax.dynamic_slice_in_dim(whole_in, place * mine, mine, 0).astype(jnp.float32)
    middle = x_tok + product_of("nht,ndh->td", mixture_tok, full_out)
    normal_two, inverse_two = statistics(middle)
    normed_two = (normal_two * gain_second).astype(jnp.bfloat16)
    widened = product_of("td,ndf->ntf", normed_two, full_in)
    gated = widened[:, :, units:]
    activated, gelu_pull = jax.vjp(exact_gelu, widened[:, :, :units])
    hidden = (activated * gated).astype(jnp.bfloat16)
    mlp_out = product_of("ntf,ndf->td", hidden, full_down)
    block_out = to_features((middle + mlp_out).astype(jnp.bfloat16))

    grad_down = product_of("td,ntf->ndf", cot_tok, hidden)
    grad_hidden = product_of("td,ndf->ntf", cot_tok, full_down)
    grad_gelu = gelu_pull(grad_hidden * gated)[0]
    grad_wide = jnp.concatenate([grad_gelu, grad_hidden * activated], axis=2).astype(jnp.bfloat16)
    grad_inner = product_of("td,ntf->ndf", normed_two, grad_wide)
    grad_norm_two = product_of("ntf,ndf->td", grad_wide, full_in)
    back_two, gain_grad_two = norm_back(grad_norm_two, normal_two, inverse_two, gain_second)
    grad_middle = cot_tok.astype(jnp.float32) + back_two
    grad_low = grad_middle.astype(jnp.bfloat16)
    grad_mixture = product_of("td,ndh->nht", grad_low, full_out).astype(jnp.bfloat16)
    grad_heads = crossed(grad_mixture).transpose(1, 0, 2).reshape(local_heads, HEAD_DIM, tokens)
    grad_attn = product_of("td,nht->ndh", grad_low, mixture_tok)
    pieces = [part[n] for n in range(2) for part in (grad_inner, grad_attn, grad_down)]
    stacked = jnp.concatenate([piece.astype(jnp.bfloat16) for piece in pieces], axis=1)
    grad_heads, stacked = lax.optimization_barrier((grad_heads, stacked))
    spread = lax.psum_scatter(stacked, "dp", scatter_dimension=0, tiled=True)
    kept, given = in_order(foremost, spread[:, : down_at + units], spread[:, down_at + units :])
    summed = kept.astype(jnp.float32) + swapped(given, "tensor", 0).astype(jnp.float32)

    query_grad, key_grad, value_grad = attend_back(
        query,
        all_keys,
        all_values,
        mixture,
        grad_heads,
        level,
        row_labels,
        column_labels,
        first,
        last,
    )

    def own_sum(both):
        early, late = both[:, :, :tokens], both[:, :, tokens:]
        away = jnp.where(leads, late, early).astype(jnp.bfloat16)
        return jnp.where(leads, early, late) + swapped(away, "dp", 0).astype(jnp.float32)

    grad_query = unturn(query_grad, cosine, sine)
    grad_key = unturn(own_sum(key_grad), cosine, sine)
    grad_proj = jnp.stack([grad_query, grad_key, own_sum(value_grad)]).astype(jnp.bfloat16)
    grad_norm_part = product_of("chxt,dchx->td", grad_proj, full_qkv).astype(jnp.bfloat16)
    kept_norm, given_norm = in_order(foremost, grad_norm_part[:mine], grad_norm_part[mine:])
    grad_norm_one = kept_norm.astype(jnp.float32) + swapped(given_norm, "tensor", 0).astype(
        jnp.float32
    )
    gain_part = jnp.sum(grad_norm_part.astype(jnp.float32) * normal_one, axis=0)
    grad_project = product_of("td,chxt->dchx", normed_one, grad_proj)
    last_grads = jnp.concatenate(
        [
            grad_project.reshape(features, 3 * headed).astype(jnp.bfloat16),
            gain_part[:, None].astype(jnp.bfloat16),
            gain_grad_two[:, None].astype(jnp.bfloat16),
        ],
        axis=1,
    )
    last_sums = lax.psum_scatter(last_grads, "dp", scatter_dimension=0, tiled=True).astype(
        jnp.float32
    )
    summed_qkv = last_sums[:, : 3 * headed]
    gain_halves = last_sums[:, 3 * headed :].T
    gain_sums = lax.dynamic_slice_in_dim(
        gain_halves + swapped(gain_halves, "tensor", 0), place * (shard // 2), shard // 2, 1
    )
    normal_tok, inverse_tok = statistics(x_tok)
    back_one, _ = norm_back(grad_norm_one, normal_tok, inverse_tok, gain_first)
    grad_in = to_features((grad_middle + back_one).astype(jnp.bfloat16))
    return (
        block_out,
        grad_in,
        summed_qkv.reshape(shard, 3, headed),
        summed[:, wide:down_at].T,
        summed[:, :wide].reshape(shard, 2, units),
        summed[:, down_at:].T,
        gain_sums[0],
        gain_sums[1],
    )


def solution(mesh):
    placed = (
        P("dp", "tensor"),
        P("dp", "tensor"),
        P("dp"),
        P("dp", None, "tensor"),
        P("tensor", "dp"),
        P("dp", None, "tensor"),
        P("tensor", "dp"),
        P("dp"),
        P("dp"),
    )
    return jax.shard_map(
        on_device,
        mesh=mesh,
        in_specs=placed,
        out_specs=(
            P("dp", "tensor"),
            P("dp", "tensor"),
            P("dp", None, "tensor"),
            P("tensor", "dp"),
            P("dp", None, "tensor"),
            P("tensor", "dp"),
            P(("dp", "tensor")),
            P(("dp", "tensor")),
        ),
        check_vma=False,
    )
```

```python
import functools

import jax
import jax.numpy as jnp
from jax import lax
from jax.experimental import pallas as pl
from jax.experimental.pallas import tpu as pltpu
from jax.sharding import PartitionSpec as P

HEAD_DIM = 64

EPS = 1e-05
THETA = 160000.0
LOG2E = 1.4426950408889634
FACTOR = HEAD_DIM**-0.5 * LOG2E
MASKED = -1e30
VMEM_BYTES = 56 * 1024 * 1024


def swapped(block, axis, stride):
    count = lax.axis_size(axis)
    route = []
    for low in range(count):
        high = low | 1 << stride
        if high != low and high < count:
            route += [(low, high), (high, low)]
    return lax.ppermute(block, axis, route)


def exact_gelu(values):
    return jax.nn.gelu(values, approximate=False)


def statistics(values):
    centre = jnp.mean(values, axis=-1, keepdims=True)
    centred = values - centre
    inverse = lax.rsqrt(jnp.mean(centred * centred, axis=-1, keepdims=True) + EPS)
    return (centred * inverse, inverse)


def rotation(length, offset):
    half = HEAD_DIM // 2
    ladder = THETA ** (-(jnp.arange(half, dtype=jnp.float32) * 2.0 / HEAD_DIM))
    places = (offset + jnp.arange(length, dtype=jnp.int32)).astype(jnp.float32)
    angle = ladder[:, None] * places[None, :]
    return (jnp.cos(angle)[None], jnp.sin(angle)[None])


def turn(values, cosine, sine):
    half = values.shape[1] // 2
    former = values[:, :half]
    latter = values[:, half:]
    return jnp.concatenate(
        [former * cosine - latter * sine, latter * cosine + former * sine], axis=1
    )


def unturn(grads, cosine, sine):
    half = grads.shape[1] // 2
    former = grads[:, :half]
    latter = grads[:, half:]
    return jnp.concatenate(
        [former * cosine + latter * sine, latter * cosine - former * sine], axis=1
    )


def product(left, right, dims):
    return lax.dot_general(left, right, (dims, ((), ())), preferred_element_type=jnp.float32)


def attend_kernel(
    first_ref, last_ref, q_ref, k_ref, v_ref, qlab_ref, klab_ref, out_ref, lse_ref, keys, *, part
):
    block = pl.program_id(1)
    heads, dim, rows = q_ref.shape

    @pl.when(block == 0)
    def _():
        for h in range(heads):
            keys[h] = k_ref[h].T

    labels = qlab_ref[...]
    queries = [q_ref[h] for h in range(heads)]

    def step(j, carry):
        start = pl.multiple_of(j * part, part)
        same = klab_ref[pl.ds(start, part), :] == labels
        state = []
        for h in range(heads):
            highest, total, mixed = carry[h]
            raw = product(keys[h, pl.ds(start, part), :], queries[h], ((1,), (0,)))
            raw = jnp.where(same, raw, MASKED)
            peak = jnp.maximum(highest, jnp.max(raw, axis=0, keepdims=True))
            fade = jnp.exp2((highest - peak) * FACTOR)
            prob = jnp.exp2(raw * FACTOR - peak * FACTOR)
            total = total * fade + jnp.sum(prob, axis=0, keepdims=True)
            mixed = mixed * fade + product(
                v_ref[h, :, pl.ds(start, part)], prob.astype(jnp.bfloat16), ((1,), (0,))
            )
            state.append((peak, total, mixed))
        return tuple(state)

    empty = tuple(
        (
            jnp.full((1, rows), MASKED, jnp.float32),
            jnp.zeros((1, rows), jnp.float32),
            jnp.zeros((dim, rows), jnp.float32),
        )
        for _ in range(heads)
    )
    result = lax.fori_loop(first_ref[block], last_ref[block], step, empty)
    for h in range(heads):
        highest, total, mixed = result[h]
        out_ref[h] = (mixed / total).astype(out_ref.dtype)
        lse_ref[h] = highest * FACTOR + jnp.log2(total)


def attend_back_kernel(
    first_ref,
    last_ref,
    q_ref,
    k_ref,
    v_ref,
    out_ref,
    grad_ref,
    lse_ref,
    qlab_ref,
    klab_ref,
    dq_ref,
    dk_ref,
    dv_ref,
    keys,
    values,
    key_grad,
    value_grad,
    *,
    part,
):
    block = pl.program_id(1)
    heads, dim, rows = q_ref.shape

    @pl.when(block == 0)
    def _():
        for h in range(heads):
            keys[h] = k_ref[h].T
            values[h] = v_ref[h].T
        key_grad[...] = jnp.zeros_like(key_grad)
        value_grad[...] = jnp.zeros_like(value_grad)

    labels = qlab_ref[...]
    queries = [q_ref[h] for h in range(heads)]
    grads = [grad_ref[h] for h in range(heads)]
    query_rows = [q.T for q in queries]
    grad_rows = [g.T for g in grads]
    levels = [lse_ref[h] for h in range(heads)]
    corrections = [
        jnp.sum(
            grads[h].astype(jnp.float32) * out_ref[h].astype(jnp.float32), axis=0, keepdims=True
        )
        for h in range(heads)
    ]

    def step(j, carry):
        start = pl.multiple_of(j * part, part)
        span = pl.ds(start, part)
        same = klab_ref[span, :] == labels
        state = []
        for h in range(heads):
            raw = product(keys[h, span, :], queries[h], ((1,), (0,)))
            grad_prob = product(values[h, span, :], grads[h], ((1,), (0,)))
            prob = jnp.exp2(jnp.where(same, raw * FACTOR - levels[h], MASKED))
            grad_score = (prob * (grad_prob - corrections[h])).astype(jnp.bfloat16)
            value_grad[h, span, :] += product(
                prob.astype(jnp.bfloat16), grad_rows[h], ((1,), (0,))
            )
            key_grad[h, span, :] += product(grad_score, query_rows[h], ((1,), (0,)))
            state.append(carry[h] + product(k_ref[h, :, span], grad_score, ((1,), (0,))))
        return tuple(state)

    empty = tuple(jnp.zeros((dim, rows), jnp.float32) for _ in range(heads))
    result = lax.fori_loop(first_ref[block], last_ref[block], step, empty)
    for h in range(heads):
        dq_ref[h] = result[h] * HEAD_DIM**-0.5

    @pl.when(block == pl.num_programs(1) - 1)
    def _():
        for h in range(heads):
            dk_ref[h] = key_grad[h].T * HEAD_DIM**-0.5
            dv_ref[h] = value_grad[h].T


def split_rows(heads, dim, rows):
    return pl.BlockSpec((heads, dim, rows), lambda h, i, *_: (h, 0, i))


def all_rows(heads, dim, rows):
    return pl.BlockSpec((heads, dim, rows), lambda h, i, *_: (h, 0, 0))


def layout_of(heads, tokens):
    together = 2 if heads % 2 == 0 else 1
    rows = min(tokens, 512)
    part = min(tokens, 512)
    return together, rows, part


def attend(query, keys, values, row_labels, column_labels, first, last):
    heads, dim, tokens = query.shape
    length = keys.shape[2]
    together, rows, part = layout_of(heads, tokens)
    cost = heads * tokens * length
    return pl.pallas_call(
        functools.partial(attend_kernel, part=part),
        grid_spec=pltpu.PrefetchScalarGridSpec(
            num_scalar_prefetch=2,
            grid=(heads // together, tokens // rows),
            in_specs=[
                split_rows(together, dim, rows),
                all_rows(together, dim, length),
                all_rows(together, dim, length),
                pl.BlockSpec((1, rows), lambda h, i, *_: (0, i)),
                pl.BlockSpec((length, 1), lambda h, i, *_: (0, 0)),
            ],
            out_specs=[split_rows(together, dim, rows), split_rows(together, 1, rows)],
            scratch_shapes=[pltpu.VMEM((together, length, dim), jnp.bfloat16)],
        ),
        out_shape=[
            jax.ShapeDtypeStruct((heads, dim, tokens), jnp.bfloat16),
            jax.ShapeDtypeStruct((heads, 1, tokens), jnp.float32),
        ],
        compiler_params=pltpu.CompilerParams(vmem_limit_bytes=VMEM_BYTES),
        cost_estimate=pl.CostEstimate(
            flops=16 * dim * cost // 2, bytes_accessed=8 * heads * dim * length, transcendentals=cost
        ),
    )(first, last, query, keys, values, row_labels, column_labels)


def attend_back(
    query, keys, values, mixture, grad, level, row_labels, column_labels, first, last
):
    heads, dim, tokens = query.shape
    length = keys.shape[2]
    together, rows, part = layout_of(heads, tokens)
    cost = heads * tokens * length
    return pl.pallas_call(
        functools.partial(attend_back_kernel, part=part),
        grid_spec=pltpu.PrefetchScalarGridSpec(
            num_scalar_prefetch=2,
            grid=(heads // together, tokens // rows),
            in_specs=[
                split_rows(together, dim, rows),
                all_rows(together, dim, length),
                all_rows(together, dim, length),
                split_rows(together, dim, rows),
                split_rows(together, dim, rows),
                split_rows(together, 1, rows),
                pl.BlockSpec((1, rows), lambda h, i, *_: (0, i)),
                pl.BlockSpec((length, 1), lambda h, i, *_: (0, 0)),
            ],
            out_specs=[
                split_rows(together, dim, rows),
                all_rows(together, dim, length),
                all_rows(together, dim, length),
            ],
            scratch_shapes=[
                pltpu.VMEM((together, length, dim), jnp.bfloat16),
                pltpu.VMEM((together, length, dim), jnp.bfloat16),
                pltpu.VMEM((together, length, dim), jnp.float32),
                pltpu.VMEM((together, length, dim), jnp.float32),
            ],
        ),
        out_shape=[
            jax.ShapeDtypeStruct((heads, dim, tokens), jnp.float32),
            jax.ShapeDtypeStruct((heads, dim, length), jnp.float32),
            jax.ShapeDtypeStruct((heads, dim, length), jnp.float32),
        ],
        compiler_params=pltpu.CompilerParams(vmem_limit_bytes=VMEM_BYTES),
        cost_estimate=pl.CostEstimate(
            flops=40 * dim * cost // 2,
            bytes_accessed=16 * heads * dim * length,
            transcendentals=cost,
        ),
    )(first, last, query, keys, values, mixture, grad, level, row_labels, column_labels)


def norm_back(grad_full, normal, inverse, gain):
    scaled = grad_full * gain
    mean_grad = jnp.mean(scaled, axis=-1, keepdims=True)
    mean_cross = jnp.mean(scaled * normal, axis=-1, keepdims=True)
    back = inverse * (scaled - mean_grad - normal * mean_cross)
    return (back, jnp.sum(grad_full * normal, axis=0))


def product_of(pattern, left, right):
    return jnp.einsum(pattern, left, right, preferred_element_type=jnp.float32)


def crossed(block):
    return lax.all_to_all(block, "tensor", split_axis=0, concat_axis=0, tiled=True)


def in_order(foremost, own, other):
    return (jnp.where(foremost, own, other), jnp.where(foremost, other, own))


def to_tokens(block):
    tokens, width = block.shape
    parts = crossed(block.reshape(2, tokens // 2, width))
    return jnp.concatenate([parts[0], parts[1]], axis=1)


def to_features(block):
    width = block.shape[1] // 2
    parts = crossed(jnp.stack([block[:, :width], block[:, width:]]))
    return parts.reshape(-1, width)


def on_device(
    block_in, cotangent, segments, w_qkv, w_attn_out, w_mlp_in, w_mlp_out, gain_attn, gain_mlp
):
    tokens, width = block_in.shape
    mine = tokens // 2
    shard = w_qkv.shape[0]
    features = 2 * width
    place = lax.axis_index("tensor")
    units = w_mlp_in.shape[2]
    headed = w_qkv.shape[2]
    local_heads = headed // HEAD_DIM
    wide, down_at = 2 * units, 2 * units + headed

    foremost = place == 0
    other_in = swapped(block_in, "tensor", 0)
    whole_in = jnp.concatenate(in_order(foremost, block_in, other_in), axis=1)
    first_weights = lax.all_gather(
        jnp.concatenate(
            [w_qkv.reshape(shard, 3 * headed), gain_attn[:, None], gain_mlp[:, None]], axis=1
        ),
        "dp",
        axis=0,
        tiled=True,
    )
    full_qkv = first_weights[:, : 3 * headed].reshape(features, 3, local_heads, HEAD_DIM)
    gain_first = first_weights[:, 3 * headed].astype(jnp.float32)
    gain_second = first_weights[:, 3 * headed + 1].astype(jnp.float32)
    half_weights = lax.all_gather(
        jnp.concatenate([w_mlp_in.reshape(shard, wide), w_attn_out.T, w_mlp_out.T], axis=1),
        "dp",
        axis=0,
        tiled=True,
    )
    other_weights = swapped(half_weights, "tensor", 0)
    both_weights = jnp.stack(in_order(foremost, half_weights, other_weights))
    full_in = both_weights[:, :, :wide]
    full_out = both_weights[:, :, wide:down_at]
    full_down = both_weights[:, :, down_at:]
    cot_tok = to_tokens(cotangent)

    half_index = lax.axis_index("dp") % 2
    normal_one, _ = statistics(whole_in.astype(jnp.float32))
    normed_one = (normal_one * gain_first).astype(jnp.bfloat16)
    projected = product_of("td,dchx->chxt", normed_one, full_qkv)
    cosine, sine = rotation(tokens, half_index * tokens)
    query = turn(projected[0], cosine, sine).astype(jnp.bfloat16)
    key_heads = turn(projected[1], cosine, sine).astype(jnp.bfloat16)
    value_heads = projected[2].astype(jnp.bfloat16)
    other_keys, other_values, other_labels = swapped((key_heads, value_heads, segments), "dp", 0)
    leads = half_index == 0

    def ordered(own, other):
        return jnp.concatenate(
            [jnp.where(leads, own, other), jnp.where(leads, other, own)], axis=-1
        )

    all_keys = ordered(key_heads, other_keys)
    all_values = ordered(value_heads, other_values)
    all_labels = ordered(segments, other_labels)
    _, rows, part = layout_of(local_heads, tokens)
    lows = segments[::rows]
    highs = segments[rows - 1 :: rows]
    below = jnp.sum((all_labels[None, :] < lows[:, None]).astype(jnp.int32), axis=1)
    within = jnp.sum((all_labels[None, :] <= highs[:, None]).astype(jnp.int32), axis=1)
    first = below // part
    last = (within + part - 1) // part
    row_labels = segments[None, :]
    column_labels = all_labels[:, None]

    mixture, level = attend(query, all_keys, all_values, row_labels, column_labels, first, last)
    mixture_halves = mixture.reshape(headed, 2, mine).transpose(1, 0, 2)
    mixture_tok = crossed(mixture_halves)
    x_tok = lax.dynamic_slice_in_dim(whole_in, place * mine, mine, 0).astype(jnp.float32)
    middle = x_tok + product_of("nht,ndh->td", mixture_tok, full_out)
    normal_two, inverse_two = statistics(middle)
    normed_two = (normal_two * gain_second).astype(jnp.bfloat16)
    widened = product_of("td,ndf->ntf", normed_two, full_in)
    gated = widened[:, :, units:]
    activated, gelu_pull = jax.vjp(exact_gelu, widened[:, :, :units])
    hidden = (activated * gated).astype(jnp.bfloat16)
    mlp_out = product_of("ntf,ndf->td", hidden, full_down)
    block_out = to_features((middle + mlp_out).astype(jnp.bfloat16))

    grad_down = product_of("td,ntf->ndf", cot_tok, hidden)
    grad_hidden = product_of("td,ndf->ntf", cot_tok, full_down)
    grad_gelu = gelu_pull(grad_hidden * gated)[0]
    grad_wide = jnp.concatenate([grad_gelu, grad_hidden * activated], axis=2).astype(jnp.bfloat16)
    grad_inner = product_of("td,ntf->ndf", normed_two, grad_wide)
    grad_norm_two = product_of("ntf,ndf->td", grad_wide, full_in)
    back_two, gain_grad_two = norm_back(grad_norm_two, normal_two, inverse_two, gain_second)
    grad_middle = cot_tok.astype(jnp.float32) + back_two
    grad_low = grad_middle.astype(jnp.bfloat16)
    grad_mixture = product_of("td,ndh->nht", grad_low, full_out).astype(jnp.bfloat16)
    grad_heads = crossed(grad_mixture).transpose(1, 0, 2).reshape(local_heads, HEAD_DIM, tokens)
    grad_attn = product_of("td,nht->ndh", grad_low, mixture_tok)
    halves = [
        jnp.concatenate([grad_inner[n], grad_attn[n], grad_down[n]], axis=1).astype(jnp.bfloat16)
        for n in range(2)
    ]
    kept, given = in_order(foremost, halves[0], halves[1])
    grad_heads, kept, given = lax.optimization_barrier((grad_heads, kept, given))
    received = swapped(given, "tensor", 0)
    halved = (kept.astype(jnp.float32) + received.astype(jnp.float32)).astype(jnp.bfloat16)
    summed = lax.psum_scatter(halved, "dp", scatter_dimension=0, tiled=True).astype(jnp.float32)

    query_grad, key_grad, value_grad = attend_back(
        query,
        all_keys,
        all_values,
        mixture,
        grad_heads,
        level,
        row_labels,
        column_labels,
        first,
        last,
    )

    def own_sum(both):
        early, late = both[:, :, :tokens], both[:, :, tokens:]
        away = jnp.where(leads, late, early).astype(jnp.bfloat16)
        return jnp.where(leads, early, late) + swapped(away, "dp", 0).astype(jnp.float32)

    grad_query = unturn(query_grad, cosine, sine)
    grad_key = unturn(own_sum(key_grad), cosine, sine)
    grad_proj = jnp.stack([grad_query, grad_key, own_sum(value_grad)]).astype(jnp.bfloat16)
    grad_norm_part = product_of("chxt,dchx->td", grad_proj, full_qkv).astype(jnp.bfloat16)
    kept_norm, given_norm = in_order(foremost, grad_norm_part[:mine], grad_norm_part[mine:])
    grad_norm_one = kept_norm.astype(jnp.float32) + swapped(given_norm, "tensor", 0).astype(
        jnp.float32
    )
    gain_part = jnp.sum(grad_norm_part.astype(jnp.float32) * normal_one, axis=0)
    grad_project = product_of("td,chxt->dchx", normed_one, grad_proj)
    last_grads = jnp.concatenate(
        [
            grad_project.reshape(features, 3 * headed).astype(jnp.bfloat16),
            gain_part[:, None].astype(jnp.bfloat16),
            gain_grad_two[:, None].astype(jnp.bfloat16),
        ],
        axis=1,
    )
    last_sums = lax.psum_scatter(last_grads, "dp", scatter_dimension=0, tiled=True).astype(
        jnp.float32
    )
    summed_qkv = last_sums[:, : 3 * headed]
    gain_halves = last_sums[:, 3 * headed :].T
    gain_sums = lax.dynamic_slice_in_dim(
        gain_halves + swapped(gain_halves, "tensor", 0), place * (shard // 2), shard // 2, 1
    )
    normal_tok, inverse_tok = statistics(x_tok)
    back_one, _ = norm_back(grad_norm_one, normal_tok, inverse_tok, gain_first)
    grad_in = to_features((grad_middle + back_one).astype(jnp.bfloat16))
    return (
        block_out,
        grad_in,
        summed_qkv.reshape(shard, 3, headed),
        summed[:, wide:down_at].T,
        summed[:, :wide].reshape(shard, 2, units),
        summed[:, down_at:].T,
        gain_sums[0],
        gain_sums[1],
    )


def solution(mesh):
    placed = (
        P("dp", "tensor"),
        P("dp", "tensor"),
        P("dp"),
        P("dp", None, "tensor"),
        P("tensor", "dp"),
        P("dp", None, "tensor"),
        P("tensor", "dp"),
        P("dp"),
        P("dp"),
    )
    return jax.shard_map(
        on_device,
        mesh=mesh,
        in_specs=placed,
        out_specs=(
            P("dp", "tensor"),
            P("dp", "tensor"),
            P("dp", None, "tensor"),
            P("tensor", "dp"),
            P("dp", None, "tensor"),
            P("tensor", "dp"),
            P(("dp", "tensor")),
            P(("dp", "tensor")),
        ),
        check_vma=False,
    )
```
